256 devices in a mesh: date: 128 (over x, y, z), col: 2 (over core).
Axes of the slice: x: 4, y: 4, z: 8, core: 2. Of those that a mesh axis runs over, the one named last changes fastest.
Arguments:
- slc: bfloat16 [2, 256, 16, 4096], P(None, 'date', None, 'col'), may hold values from -6 to 6
- partner_offsets: int32 [256, 24], replicated, may hold values from 0 to 50, as said below
Outputs:
- linked: float32 [2, 4, 256, 256], P(None, None, ('date', 'col'))
The draws below stay inside these ranges and needn't reach their ends.
Inputs may be any that keep to these rules, and one draw needn't show every extreme that they name: `partner_offsets`: live slots of a date come first; its live offsets are distinct and lead to dates inside the stack; some date has 24 live slots, and the largest possible offset is used.
All inputs are finite; a program needn't handle non-finite values.
Results may differ from the reference program's by a relative error of at most 0.00045.
Values may be sent and summed in bfloat16 or wider, within the bound.
A program may use at most 128 MiB of HBM per device.

```python
import jax
import jax.numpy as jnp
from jax import lax

DATES = 256
ROWS = 16
PIX_DEV = 4
WIN = 50
KMAX = 24
KMIN = 6
ITERS = 20
COLS = 4096
N_COL = 2


def draw_partner_offsets(key, part):
    key = jax.random.fold_in(key, 11)
    key_order = jax.random.fold_in(key, 1)
    key_count = jax.random.fold_in(key, 2)
    date_index = jnp.arange(DATES, dtype=jnp.int32)
    ranking = jax.vmap(lambda sub: jax.random.permutation(sub, WIN))(jax.random.split(key_order, DATES)).astype(jnp.int32)
    offset_row = jnp.arange(1, WIN + 1, dtype=jnp.int32)
    avail = jnp.minimum(WIN, DATES - 1 - date_index)
    scores = jnp.where(offset_row[None, :] <= avail[:, None], ranking, ranking + WIN)
    forced = (date_index[:, None] == 0) & (offset_row[None, :] == avail[:, None])
    scores = jnp.where(forced, -1, scores)
    order = jnp.argsort(scores, axis=1, stable=True)[:, :KMAX].astype(jnp.int32)
    counts = jax.random.randint(key_count, (DATES,), KMIN, KMAX + 1).astype(jnp.int32)
    counts = jnp.where(date_index == 0, KMAX, counts)
    live_count = jnp.minimum(counts, avail)
    slot_index = jnp.arange(KMAX, dtype=jnp.int32)
    return jnp.where(slot_index[None, :] < live_count[:, None], order + 1, 0).astype(jnp.int32)


def shard_levels(stream_key, dims, cuts, least, high):
    gain = 1.0
    for position, parts in cuts:
        heights = jax.random.uniform(jax.random.fold_in(jax.random.fold_in(stream_key, 6), position), (parts,), jnp.float32, least / len(cuts), high / len(cuts))
        gain = gain * jnp.repeat(jnp.exp(heights), dims[position] // parts).reshape((-1,) + (1,) * (len(dims) - 1 - position))
    return gain


def noise(own_key, dims, width, reach, shards=(), kind=jnp.bfloat16):
    result = jax.random.normal(own_key, dims, jnp.float32) * width
    if len(shards) > 0:
        result = shard_levels(own_key, dims, shards, -0.22, 0.18) * result
    return jnp.clip(result, min=-reach, max=reach).astype(kind)


def setup_inputs(seed: int = 0) -> dict:
    key_of = jax.random.split(jax.random.key(seed), 3)
    return {
        "slc": noise(key_of[0], (2, DATES, ROWS, COLS), 1.0, 6.0, ((1, 128), (3, 2))),
        "partner_offsets": draw_partner_offsets(jax.random.fold_in(key_of[2], 71), 0),
    }


epsilon = 1e-06
highest = lax.Precision.HIGHEST

def box_mean(values):
    layout = values.shape
    grouped = values.reshape(layout[:-2] + (layout[-2] // 4, 4, layout[-1] // 16, 16))
    return lax.optimization_barrier(jnp.sum(grouped, axis=(-3, -1))) / 64.0

def power_link(upper_real, upper_imag):
    date_count = upper_real.shape[-1]
    identity = jnp.eye(date_count, dtype=jnp.float32)
    herm_real = identity + upper_real + jnp.swapaxes(upper_real, -1, -2)
    herm_imag = upper_imag - jnp.swapaxes(upper_imag, -1, -2)
    start_real = jnp.ones(upper_real.shape[:-1], jnp.float32)
    start_imag = jnp.zeros(upper_real.shape[:-1], jnp.float32)

    def advance(counter, vector):
        vec_real, vec_imag = vector
        new_real = jnp.einsum('...ij,...j->...i', herm_real, vec_real, precision=highest) - jnp.einsum('...ij,...j->...i', herm_imag, vec_imag, precision=highest)
        new_imag = jnp.einsum('...ij,...j->...i', herm_real, vec_imag, precision=highest) + jnp.einsum('...ij,...j->...i', herm_imag, vec_real, precision=highest)
        factor = lax.rsqrt(lax.optimization_barrier(jnp.mean(new_real * new_real + new_imag * new_imag, axis=-1, keepdims=True)) + epsilon)
        return (new_real * factor, new_imag * factor)
    return lax.fori_loop(0, ITERS, advance, (start_real, start_imag))

def reference(slc, partner_offsets):
    date_count = slc.shape[1]
    looked_rows = ROWS // 4
    looked_cols = COLS // 16
    block_width = PIX_DEV * 4 // ROWS * N_COL
    block_count = looked_cols // block_width
    live = partner_offsets > 0
    target = jnp.arange(date_count, dtype=jnp.int32)[:, None] + partner_offsets
    partner = jnp.where(live, target, 0).astype(jnp.int32)
    onehot = jnp.where(live[:, :, None] & (target[:, :, None] == jnp.arange(date_count, dtype=jnp.int32)[None, None, :]), 1.0, 0.0).astype(jnp.float32)

    def one_block(block_index):
        start = (block_index * block_width * 16).astype(jnp.int32)
        piece = lax.dynamic_slice_in_dim(slc, start, block_width * 16, axis=3).astype(jnp.float32)
        intensity = box_mean(piece[0] * piece[0] + piece[1] * piece[1])
        partner_real = piece[0][partner]
        partner_imag = piece[1][partner]
        own_real = piece[0][:, None]
        own_imag = piece[1][:, None]
        numer_real = box_mean(own_real * partner_real + own_imag * partner_imag)
        numer_imag = box_mean(own_imag * partner_real - own_real * partner_imag)
        denom = jnp.sqrt((intensity[:, None] + epsilon) * (intensity[partner] + epsilon))
        coh_real = jnp.where(live[:, :, None, None], numer_real / denom, 0.0)
        coh_imag = jnp.where(live[:, :, None, None], numer_imag / denom, 0.0)
        upper_real = jnp.einsum('iklq,ikj->lqij', coh_real, onehot, precision=highest)
        upper_imag = jnp.einsum('iklq,ikj->lqij', coh_imag, onehot, precision=highest)
        vec_real, vec_imag = power_link(upper_real, upper_imag)
        return jnp.stack([vec_real, vec_imag])
    blocks = lax.map(one_block, jnp.arange(block_count, dtype=jnp.int32))
    return jnp.transpose(blocks, (1, 2, 0, 3, 4)).reshape(2, looked_rows, block_count * block_width, date_count)
```

```python
import functools

import jax
import jax.numpy as jnp
from jax import lax
from jax.experimental import pallas as pl
from jax.experimental.pallas import tpu as pltpu
from jax.sharding import PartitionSpec as P

EPSILON = 1e-06
BLOCKS = 5
MESH = pl.DeviceIdType.MESH


def halves(value):
    high = value.astype(jnp.bfloat16)
    low = (value - high.astype(jnp.float32)).astype(jnp.bfloat16)
    return high, low


def product(left, right):
    return jnp.dot(left, right, preferred_element_type=jnp.float32)


def gram(left, right):
    return lax.dot_general(left, right, (((1,), (1,)), ((), ())), preferred_element_type=jnp.float32)


def squared(real, imag):
    real_high, real_low = real
    imag_high, imag_low = imag
    cross = product(real_high, real_low) - product(imag_high, imag_low)
    out_real = product(real_high, real_high) - product(imag_high, imag_high) + (cross + cross.T)
    mixed = product(real_high, imag_high) + product(real_high, imag_low) + product(real_low, imag_high)
    return out_real, mixed - mixed.T


def applied(real, imag, rows):
    count = rows.shape[0]
    high, low = halves(rows)
    stacked = jnp.concatenate([high, low], axis=0)
    by_real = product(stacked, real[0])
    by_imag = product(stacked, imag[0])
    by_real = by_real[:count] + by_real[count:] + product(high, real[1])
    by_imag = by_imag[:count] + by_imag[count:] + product(high, imag[1])
    half = count // 2
    return jnp.concatenate([by_real[:half] + by_imag[half:], by_real[half:] - by_imag[:half]], axis=0)


def power_mean(rows):
    half = rows.shape[0] // 2
    squares = rows[:half] * rows[:half] + rows[half:] * rows[half:]
    return jnp.mean(squares, axis=1, keepdims=True)


def linked_phase(images, pairs):
    dates = images.shape[0]
    turned = jnp.concatenate([images[:, 64:], -images[:, :64]], axis=1)
    cov_real = gram(images, images) * (1.0 / 64.0)
    cov_imag = gram(turned, images) * (1.0 / 64.0)
    row = lax.broadcasted_iota(jnp.int32, (dates, dates), 0)
    col = lax.broadcasted_iota(jnp.int32, (dates, dates), 1)
    diagonal = row == col
    only = jnp.where(diagonal, cov_real, 0.0)
    scale_row = lax.rsqrt(jnp.sum(only, axis=0, keepdims=True) + EPSILON)
    scale_col = lax.rsqrt(jnp.sum(only, axis=1, keepdims=True) + EPSILON)
    weight = pairs * scale_row * scale_col
    herm_real = jnp.where(diagonal, 1.0, cov_real * weight)
    herm_imag = cov_imag * weight
    first = halves(herm_real), halves(herm_imag)
    square = squared(*first)
    second = halves(square[0]), halves(square[1])
    fourth = squared(*second)
    fourth = halves(fourth[0]), halves(fourth[1])

    ones = jnp.ones((1, dates), jnp.float32)
    none = jnp.zeros((1, dates), jnp.float32)
    pad = jnp.zeros((6, dates), jnp.float32)
    start = jnp.concatenate([ones, none, pad], axis=0)
    start = jnp.concatenate([ones, jnp.zeros((7, dates), jnp.float32)], axis=0)
    one = applied(*first, start)
    pair = jnp.concatenate([ones, one[0:1], none, none, none, one[4:5], none, none], axis=0)
    later = applied(*second, pair)
    rows = jnp.concatenate([ones, one[0:1], later[0:2], none, one[4:5], later[4:6]], axis=0)
    for _ in range(BLOCKS):
        after = applied(*fourth, rows)
        means = power_mean(rows)
        ratio = 1.0
        for step in (1, 2, 3):
            ratio = ratio * lax.rsqrt(ratio * ratio * means[step : step + 1] + EPSILON)
        ratio = ratio * lax.rsqrt(ratio * ratio * power_mean(after)[0:1] + EPSILON)
        rows = after * ratio
    return rows[0:1], rows[4:5]


def pair_mask(offsets):
    dates, slots = offsets.shape
    row = lax.broadcasted_iota(jnp.int32, (dates, dates), 0)
    col = lax.broadcasted_iota(jnp.int32, (dates, dates), 1)
    apart = jnp.where(col > row, col - row, -1)
    upper = jnp.zeros((dates, dates), jnp.float32)
    for slot in range(slots):
        upper = jnp.where(offsets[:, slot : slot + 1] == apart, 1.0, upper)
    return upper + upper.T


def kernel(
    groups,
    slc_ref,
    offsets_ref,
    out_ref,
    strip,
    table,
    wide,
    outgoing,
    arrived,
    ordered,
    strip_sem,
    table_sem,
    send_sem,
    recv_sem,
):
    date = lax.axis_index("date")
    core = lax.axis_index("col")
    chunks = outgoing.shape[0]
    owners = chunks // 2
    side = date // owners
    own = side == core

    barrier = pltpu.get_barrier_semaphore()

    def greet(step, carry):
        source = lax.rem(date + step, groups)

        @pl.when(jnp.logical_not((step == 0) & own))
        def _():
            pl.semaphore_signal(barrier, inc=1, device_id=(source, side), device_id_type=MESH)

        return carry

    load_strip = pltpu.make_async_copy(slc_ref, strip, strip_sem)
    load_strip.start()
    load_table = pltpu.make_async_copy(offsets_ref, table, table_sem)
    load_table.start()
    lax.fori_loop(0, groups, greet, 0)

    load_strip.wait()
    lane = lax.broadcasted_iota(jnp.int32, (8, 128), 1)

    def regroup(tile, carry):
        columns = pl.ds(pl.multiple_of(tile * 128, 128), 128)
        for part in range(2):
            for t in range(2):
                wide[tile, pl.ds(part * 32 + t * 16, 16), :] = strip[part, t, :, columns].astype(jnp.float32)
        group = [wide[tile, pl.ds((g // 4) * 32 + g % 4, 8, stride=4), :] for g in range(8)]
        for bit in range(3):
            shift = 16 << bit
            upper = (lane & shift) != 0
            for g in range(8):
                other = g | (1 << bit)
                if other != g:
                    low, high = group[g], group[other]
                    group[g] = jnp.where(upper, pltpu.roll(high, shift, 1), low)
                    group[other] = jnp.where(upper, high, pltpu.roll(low, 128 - shift, 1))
        for g in range(8):
            outgoing[tile * 8 + g] = group[g].astype(jnp.bfloat16)
        return carry

    lax.fori_loop(0, chunks // 8, regroup, 0)

    pl.semaphore_wait(barrier, jnp.where(own, chunks - 1, chunks))

    def send(step, carry):
        chunk = lax.rem(2 * date + step, chunks)
        owner = owners * core + chunk // 2
        owner_core = lax.rem(chunk, 2)
        stays = (owner == date) & (owner_core == core)

        @pl.when(jnp.logical_not(stays))
        def _():
            pltpu.make_async_remote_copy(
                src_ref=outgoing.at[chunk],
                dst_ref=arrived.at[date],
                send_sem=send_sem,
                recv_sem=recv_sem,
                device_id=(owner, owner_core),
                device_id_type=MESH,
            ).start()

        @pl.when(stays)
        def _():
            pltpu.make_async_copy(outgoing.at[chunk], arrived.at[date], recv_sem).start()

        return carry

    lax.fori_loop(0, chunks, send, 0)

    load_table.wait()
    pairs = pair_mask(table[...])

    pltpu.make_async_copy(arrived, arrived, recv_sem).wait()
    wide_rows = arrived[...].astype(jnp.float32).reshape(groups * 8, 128)
    ordered[0 : groups * 8, :] = wide_rows
    for pixel in range(4):
        for t in range(2):
            picked = ordered[pl.ds(t * 4 + pixel, groups, stride=8), :]
            ordered[pl.ds(groups * 8 + pixel * 2 * groups + t, groups, stride=2), :] = picked
    for pixel in range(4):
        first = groups * 8 + pixel * 2 * groups
        images = ordered[first : first + 2 * groups, :].astype(jnp.bfloat16)
        real, imag = linked_phase(images, pairs)
        out_ref[0, pixel] = real
        out_ref[1, pixel] = imag

    @pl.when(own)
    def _():
        rest = outgoing.at[pl.ds(0, chunks - 1)]
        pltpu.make_async_copy(rest, rest, send_sem).wait()

    @pl.when(jnp.logical_not(own))
    def _():
        pltpu.make_async_copy(outgoing, outgoing, send_sem).wait()


def solution(mesh):
    groups = mesh.shape["date"]

    def on_device(slc, partner_offsets):
        dates = slc.shape[1] * groups
        chunks = slc.shape[3] // 16
        return pl.pallas_call(
            functools.partial(kernel, groups),
            out_shape=jax.ShapeDtypeStruct((2, 4, 1, dates), jnp.float32),
            in_specs=[pl.BlockSpec(memory_space=pl.ANY)] * 2,
            out_specs=pl.BlockSpec(memory_space=pltpu.VMEM),
            scratch_shapes=[
                pltpu.VMEM(slc.shape, jnp.bfloat16),
                pltpu.VMEM(partner_offsets.shape, jnp.int32),
                pltpu.VMEM((chunks // 8, 64, 128), jnp.float32),
                pltpu.VMEM((chunks, 8, 128), jnp.bfloat16),
                pltpu.VMEM((groups, 8, 128), jnp.bfloat16),
                pltpu.VMEM((groups * 8 + 4 * dates, 128), jnp.float32),
                pltpu.SemaphoreType.DMA,
                pltpu.SemaphoreType.DMA,
                pltpu.SemaphoreType.DMA,
                pltpu.SemaphoreType.DMA,
            ],
            compiler_params=pltpu.CompilerParams(
                collective_id=0, has_side_effects=True, vmem_limit_bytes=48 * 1024 * 1024
            ),
        )(slc, partner_offsets)

    return jax.shard_map(
        on_device,
        mesh=mesh,
        in_specs=(P(None, "date", None, "col"), P()),
        out_specs=P(None, None, ("date", "col"), None),
        check_vma=False,
    )
```

```python
import functools

import jax
import jax.numpy as jnp
from jax import lax
from jax.experimental import pallas as pl
from jax.experimental.pallas import tpu as pltpu
from jax.sharding import PartitionSpec as P

EPSILON = 1e-06
STRIDES = 4
VMEM_BYTES = 56_545_280
MESH = pl.DeviceIdType.MESH


def halves(value):
    high = value.astype(jnp.bfloat16)
    low = (value - high.astype(jnp.float32)).astype(jnp.bfloat16)
    return high, low


def product(left, right):
    return jnp.dot(left, right, preferred_element_type=jnp.float32)


def gram(left, right):
    return lax.dot_general(left, right, (((1,), (1,)), ((), ())), preferred_element_type=jnp.float32)


def squared(real, imag):
    real_high, real_low = halves(real)
    imag_high, imag_low = halves(imag)
    cross = product(real_high, real_low) - product(imag_high, imag_low)
    out_real = product(real_high, real_high) - product(imag_high, imag_high) + (cross + cross.T)
    mixed = product(real_high, imag_high) + product(real_high, imag_low) + product(real_low, imag_high)
    return out_real, mixed - mixed.T


def applied(real, imag, rows):
    count = rows.shape[0]
    half = count // 2
    high, low = halves(rows)
    stacked = jnp.concatenate([high, low], axis=0)
    by_real = product(stacked, real[0])
    by_imag = product(stacked, imag[0])
    by_real = by_real[:count] + by_real[count:] + product(high, real[1])
    by_imag = by_imag[:count] + by_imag[count:] + product(high, imag[1])
    return jnp.concatenate([by_real[:half] + by_imag[half:], by_real[half:] - by_imag[:half]], axis=0)


def coherences(images, pairs, diagonal):
    turned = jnp.concatenate([images[:, 64:], -images[:, :64]], axis=1)
    cov_real = gram(images, images) * (1.0 / 64.0)
    cov_imag = gram(turned, images) * (1.0 / 64.0)
    only = jnp.where(diagonal, cov_real, 0.0)
    scale_row = lax.rsqrt(jnp.sum(only, axis=0, keepdims=True) + EPSILON)
    scale_col = lax.rsqrt(jnp.sum(only, axis=1, keepdims=True) + EPSILON)
    weight = pairs * scale_row * scale_col
    return jnp.where(diagonal, 1.0, cov_real * weight), cov_imag * weight


def times_ones(real, imag):
    return jnp.sum(real, axis=0, keepdims=True), -jnp.sum(imag, axis=0, keepdims=True)


def mean_product(a, b):
    return jnp.mean(a[0] * b[0] + a[1] * b[1], axis=1, keepdims=True)


def folded(tail, means):
    for mean in means:
        tail = mean + EPSILON * tail
    return tail


def linked_phases(images, pairs):
    dates = pairs.shape[0]
    row = lax.broadcasted_iota(jnp.int32, (dates, dates), 0)
    col = lax.broadcasted_iota(jnp.int32, (dates, dates), 1)
    first = [coherences(image, pairs, row == col) for image in images]
    second = [squared(*matrix) for matrix in first]
    two = [times_ones(*matrix) for matrix in second]
    fourth = [squared(*matrix) for matrix in second]
    four = [times_ones(*matrix) for matrix in fourth]
    fourth = [(halves(real), halves(imag)) for real, imag in fourth]
    ones = jnp.ones((1, dates), jnp.float32), jnp.zeros((1, dates), jnp.float32)
    pad = jnp.zeros((2, dates), jnp.float32)
    rows = []
    for a, b in zip(two, four):
        means = [mean_product(ones, a), mean_product(a, a), mean_product(a, b), mean_product(b, b)]
        value = jnp.concatenate([b[0], a[0], pad, b[1], a[1], pad], axis=0)
        rows.append(value * lax.rsqrt(folded(1.0, means)))
    for _ in range(STRIDES):
        after = [applied(*matrix, value) for matrix, value in zip(fourth, rows)]
        for pixel in range(len(rows)):
            old, new = rows[pixel], after[pixel]
            k = old[0:1], old[4:5]
            a, b = (new[1:2], new[5:6]), (new[0:1], new[4:5])
            means = [mean_product(k, a), mean_product(a, a), mean_product(a, b), mean_product(b, b)]
            rows[pixel] = new * lax.rsqrt(folded(1.0, means))
    return [(value[0:1], value[4:5]) for value in rows]


def pair_mask(offsets):
    slots, dates = offsets.shape
    row = lax.broadcasted_iota(jnp.int32, (dates, dates), 0)
    col = lax.broadcasted_iota(jnp.int32, (dates, dates), 1)
    apart = jnp.where(row > col, row - col, -1)
    lower = jnp.zeros((dates, dates), jnp.float32)
    for slot in range(slots):
        lower = jnp.where(offsets[slot : slot + 1, :] == apart, 1.0, lower)
    return lower + lower.T


def kernel(
    groups,
    slc_ref,
    offsets_ref,
    out_ref,
    strip,
    table,
    wide,
    outgoing,
    arrived,
    ordered,
    strip_sem,
    table_sem,
    send_sem,
    recv_sem,
):
    date = lax.axis_index("date")
    core = lax.axis_index("col")
    chunks = outgoing.shape[0]
    owners = chunks // 2
    side = date // owners
    own = side == core

    barrier = pltpu.get_barrier_semaphore()

    def greet(step, carry):
        source = lax.rem(date + step, groups)

        @pl.when(jnp.logical_not((step == 0) & own))
        def _():
            pl.semaphore_signal(barrier, inc=1, device_id=(source, side), device_id_type=MESH)

        return carry

    load_strip = pltpu.make_async_copy(slc_ref, strip, strip_sem)
    load_strip.start()
    load_table = pltpu.make_async_copy(offsets_ref, table, table_sem)
    load_table.start()
    lax.fori_loop(0, groups, greet, 0)

    load_strip.wait()
    lane = lax.broadcasted_iota(jnp.int32, (8, 128), 1)

    def regroup(tile, carry):
        columns = pl.ds(pl.multiple_of(tile * 128, 128), 128)
        for part in range(2):
            for t in range(2):
                wide[tile, pl.ds(part * 32 + t * 16, 16), :] = strip[part, t, :, columns].astype(jnp.float32)
        group = [wide[tile, pl.ds((g // 4) * 32 + g % 4, 8, stride=4), :] for g in range(8)]
        for bit in range(3):
            shift = 16 << bit
            upper = (lane & shift) != 0
            for g in range(8):
                other = g | (1 << bit)
                if other != g:
                    low, high = group[g], group[other]
                    group[g] = jnp.where(upper, pltpu.roll(high, shift, 1), low)
                    group[other] = jnp.where(upper, high, pltpu.roll(low, 128 - shift, 1))
        for g in range(8):
            outgoing[tile * 8 + g] = group[g].astype(jnp.bfloat16)
        return carry

    lax.fori_loop(0, chunks // 8, regroup, 0)

    pl.semaphore_wait(barrier, jnp.where(own, chunks - 1, chunks))

    def send(step, carry):
        chunk = lax.rem(2 * date + step, chunks)
        owner = owners * core + chunk // 2
        owner_core = lax.rem(chunk, 2)
        stays = (owner == date) & (owner_core == core)

        @pl.when(jnp.logical_not(stays))
        def _():
            pltpu.make_async_remote_copy(
                src_ref=outgoing.at[chunk],
                dst_ref=arrived.at[date],
                send_sem=send_sem,
                recv_sem=recv_sem,
                device_id=(owner, owner_core),
                device_id_type=MESH,
            ).start()

        @pl.when(stays)
        def _():
            pltpu.make_async_copy(outgoing.at[chunk], arrived.at[date], recv_sem).start()

        return carry

    lax.fori_loop(0, chunks, send, 0)

    load_table.wait()
    pairs = pair_mask(table[...])

    pltpu.make_async_copy(arrived, arrived, recv_sem).wait()
    wide_rows = arrived[...].astype(jnp.float32).reshape(groups * 8, 128)
    ordered[0 : groups * 8, :] = wide_rows
    for pixel in range(4):
        for t in range(2):
            picked = ordered[pl.ds(t * 4 + pixel, groups, stride=8), :]
            ordered[pl.ds(groups * 8 + pixel * 2 * groups + t, groups, stride=2), :] = picked
    images = []
    for pixel in range(4):
        first = groups * 8 + pixel * 2 * groups
        images.append(ordered[first : first + 2 * groups, :].astype(jnp.bfloat16))
    for pixel, (real, imag) in enumerate(linked_phases(images, pairs)):
        out_ref[0, pixel] = real
        out_ref[1, pixel] = imag

    @pl.when(own)
    def _():
        rest = outgoing.at[pl.ds(0, chunks - 1)]
        pltpu.make_async_copy(rest, rest, send_sem).wait()

    @pl.when(jnp.logical_not(own))
    def _():
        pltpu.make_async_copy(outgoing, outgoing, send_sem).wait()


def solution(mesh):
    groups = mesh.shape["date"]

    def on_device(slc, partner_offsets):
        dates = slc.shape[1] * groups
        chunks = slc.shape[3] // 16
        return pl.pallas_call(
            functools.partial(kernel, groups),
            out_shape=jax.ShapeDtypeStruct((2, 4, 1, dates), jnp.float32),
            in_specs=[pl.BlockSpec(memory_space=pltpu.HBM)] * 2,
            out_specs=pl.BlockSpec(memory_space=pltpu.VMEM),
            scratch_shapes=[
                pltpu.VMEM(slc.shape, jnp.bfloat16),
                pltpu.VMEM(partner_offsets.shape[::-1], jnp.int32),
                pltpu.VMEM((chunks // 8, 64, 128), jnp.float32),
                pltpu.VMEM((chunks, 8, 128), jnp.bfloat16),
                pltpu.VMEM((groups, 8, 128), jnp.bfloat16),
                pltpu.VMEM((groups * 8 + 4 * dates, 128), jnp.float32),
                pltpu.SemaphoreType.DMA,
                pltpu.SemaphoreType.DMA,
                pltpu.SemaphoreType.DMA,
                pltpu.SemaphoreType.DMA,
            ],
            compiler_params=pltpu.CompilerParams(
                collective_id=0, has_side_effects=True, vmem_limit_bytes=VMEM_BYTES
            ),
        )(slc, partner_offsets.T)

    return jax.shard_map(
        on_device,
        mesh=mesh,
        in_specs=(P(None, "date", None, "col"), P()),
        out_specs=P(None, None, ("date", "col"), None),
        check_vma=False,
    )
```

```python
import functools

import jax
import jax.numpy as jnp
from jax import lax
from jax.experimental import pallas as pl
from jax.experimental.pallas import tpu as pltpu
from jax.sharding import PartitionSpec as P

EPSILON = 1e-06
STRIDES = 4
VMEM_BYTES = 56_545_280
DEPTH = 8
MESH = pl.DeviceIdType.MESH


def halves(value):
    high = value.astype(jnp.bfloat16)
    low = (value - high.astype(jnp.float32)).astype(jnp.bfloat16)
    return high, low


def product(left, right):
    return jnp.dot(left, right, preferred_element_type=jnp.float32)


def gram(left, right):
    return lax.dot_general(left, right, (((1,), (1,)), ((), ())), preferred_element_type=jnp.float32)


def squared(real, imag):
    real_high, real_low = halves(real)
    imag_high, imag_low = halves(imag)
    cross = product(real_high, real_low) - product(imag_high, imag_low)
    out_real = product(real_high, real_high) - product(imag_high, imag_high) + (cross + cross.T)
    mixed = product(real_high, imag_high) + product(real_high, imag_low) + product(real_low, imag_high)
    return out_real, mixed - mixed.T


def applied(real, imag, rows):
    count = rows.shape[0]
    half = count // 2
    high, low = halves(rows)
    stacked = jnp.concatenate([high, low], axis=0)
    by_real = product(stacked, real[0])
    by_imag = product(stacked, imag[0])
    by_real = by_real[:count] + by_real[count:] + product(high, real[1])
    by_imag = by_imag[:count] + by_imag[count:] + product(high, imag[1])
    return jnp.concatenate([by_real[:half] + by_imag[half:], by_real[half:] - by_imag[:half]], axis=0)


def coherences(images, pairs, diagonal):
    turned = jnp.concatenate([images[:, 64:], -images[:, :64]], axis=1)
    cov_real = gram(images, images) * (1.0 / 64.0)
    cov_imag = gram(turned, images) * (1.0 / 64.0)
    only = jnp.where(diagonal, cov_real, 0.0)
    scale_row = lax.rsqrt(jnp.sum(only, axis=0, keepdims=True) + EPSILON)
    scale_col = lax.rsqrt(jnp.sum(only, axis=1, keepdims=True) + EPSILON)
    weight = pairs * scale_row * scale_col
    return jnp.where(diagonal, 1.0, cov_real * weight), cov_imag * weight


def times_ones(real, imag):
    return jnp.sum(real, axis=0, keepdims=True), -jnp.sum(imag, axis=0, keepdims=True)


def mean_product(a, b):
    return jnp.mean(a[0] * b[0] + a[1] * b[1], axis=1, keepdims=True)


def folded(tail, means):
    for mean in means:
        tail = mean + EPSILON * tail
    return tail


def linked_phases(images, pairs):
    dates = pairs.shape[0]
    row = lax.broadcasted_iota(jnp.int32, (dates, dates), 0)
    col = lax.broadcasted_iota(jnp.int32, (dates, dates), 1)
    first = [coherences(image, pairs, row == col) for image in images]
    second = [squared(*matrix) for matrix in first]
    two = [times_ones(*matrix) for matrix in second]
    fourth = [squared(*matrix) for matrix in second]
    four = [times_ones(*matrix) for matrix in fourth]
    fourth = [(halves(real), halves(imag)) for real, imag in fourth]
    ones = jnp.ones((1, dates), jnp.float32), jnp.zeros((1, dates), jnp.float32)
    pad = jnp.zeros((2, dates), jnp.float32)
    rows = []
    for a, b in zip(two, four):
        means = [mean_product(ones, a), mean_product(a, a), mean_product(a, b), mean_product(b, b)]
        value = jnp.concatenate([b[0], a[0], pad, b[1], a[1], pad], axis=0)
        rows.append(value * lax.rsqrt(folded(1.0, means)))
    for _ in range(STRIDES):
        after = [applied(*matrix, value) for matrix, value in zip(fourth, rows)]
        for pixel in range(len(rows)):
            old, new = rows[pixel], after[pixel]
            k = old[0:1], old[4:5]
            a, b = (new[1:2], new[5:6]), (new[0:1], new[4:5])
            means = [mean_product(k, a), mean_product(a, a), mean_product(a, b), mean_product(b, b)]
            rows[pixel] = new * lax.rsqrt(folded(1.0, means))
    return [(value[0:1], value[4:5]) for value in rows]


def pair_mask(offsets):
    slots, dates = offsets.shape
    row = lax.broadcasted_iota(jnp.int32, (dates, dates), 0)
    col = lax.broadcasted_iota(jnp.int32, (dates, dates), 1)
    apart = jnp.where(row > col, row - col, -1)
    lower = jnp.zeros((dates, dates), jnp.float32)
    for slot in range(slots):
        lower = jnp.where(offsets[slot : slot + 1, :] == apart, 1.0, lower)
    return lower + lower.T


def kernel(
    groups,
    slc_ref,
    offsets_ref,
    out_ref,
    strip,
    table,
    wide,
    outgoing,
    arrived,
    ordered,
    strip_sem,
    table_sem,
    send_sem,
    recv_sem,
):
    date = lax.axis_index("date")
    core = lax.axis_index("col")
    chunks = outgoing.shape[0]
    owners = chunks // 2
    side = date // owners
    own = side == core

    barrier = pltpu.get_barrier_semaphore()

    def greet(step, carry):
        source = lax.rem(date + step, groups)
        pl.semaphore_signal(barrier, inc=1, device_id=(source, side), device_id_type=MESH)
        return carry

    load_strip = pltpu.make_async_copy(slc_ref, strip, strip_sem)
    load_strip.start()
    load_table = pltpu.make_async_copy(offsets_ref, table, table_sem)
    load_table.start()
    lax.fori_loop(1, groups, greet, 0)

    @pl.when(jnp.logical_not(own))
    def _():
        greet(0, 0)


    load_strip.wait()
    lane = lax.broadcasted_iota(jnp.int32, (8, 128), 1)

    def regroup(tile, carry):
        columns = pl.ds(pl.multiple_of(tile * 128, 128), 128)
        for part in range(2):
            for t in range(2):
                wide[tile, pl.ds(part * 32 + t * 16, 16), :] = strip[part, t, :, columns].astype(jnp.float32)
        group = [wide[tile, pl.ds((g // 4) * 32 + g % 4, 8, stride=4), :] for g in range(8)]
        for bit in range(3):
            shift = 16 << bit
            upper = (lane & shift) != 0
            for g in range(8):
                other = g | (1 << bit)
                if other != g:
                    low, high = group[g], group[other]
                    group[g] = jnp.where(upper, pltpu.roll(high, shift, 1), low)
                    group[other] = jnp.where(upper, high, pltpu.roll(low, 128 - shift, 1))
        for g in range(8):
            outgoing[tile * 8 + g] = group[g].astype(jnp.bfloat16)
        return carry

    lax.fori_loop(0, chunks // 8, regroup, 0, unroll=8)

    pl.semaphore_wait(barrier, jnp.where(own, chunks - 1, chunks))

    def send(step, carry):
        y, z, x = lax.rem(step // 2, 4), lax.rem(step // 8, DEPTH), step // (8 * DEPTH)
        chunk = ((x * 4 + y) * DEPTH + z) * 2 + lax.rem(step, 2)
        owner = owners * core + chunk // 2
        owner_core = lax.rem(chunk, 2)
        stays = (owner == date) & (owner_core == core)

        @pl.when(jnp.logical_not(stays))
        def _():
            pltpu.make_async_remote_copy(
                src_ref=outgoing.at[chunk],
                dst_ref=arrived.at[date],
                send_sem=send_sem,
                recv_sem=recv_sem,
                device_id=(owner, owner_core),
                device_id_type=MESH,
            ).start()

        @pl.when(stays)
        def _():
            pltpu.make_async_copy(outgoing.at[chunk], arrived.at[date], recv_sem).start()

        return carry

    lax.fori_loop(0, chunks, send, 0)

    load_table.wait()
    pairs = pair_mask(table[...])

    pltpu.make_async_copy(arrived, arrived, recv_sem).wait()
    wide_rows = arrived[...].astype(jnp.float32).reshape(groups * 8, 128)
    ordered[0 : groups * 8, :] = wide_rows
    for pixel in range(4):
        for t in range(2):
            picked = ordered[pl.ds(t * 4 + pixel, groups, stride=8), :]
            ordered[pl.ds(groups * 8 + pixel * 2 * groups + t, groups, stride=2), :] = picked
    images = []
    for pixel in range(4):
        first = groups * 8 + pixel * 2 * groups
        images.append(ordered[first : first + 2 * groups, :].astype(jnp.bfloat16))
    for pixel, (real, imag) in enumerate(linked_phases(images, pairs)):
        out_ref[0, pixel] = real
        out_ref[1, pixel] = imag

    @pl.when(own)
    def _():
        rest = outgoing.at[pl.ds(0, chunks - 1)]
        pltpu.make_async_copy(rest, rest, send_sem).wait()

    @pl.when(jnp.logical_not(own))
    def _():
        pltpu.make_async_copy(outgoing, outgoing, send_sem).wait()


def solution(mesh):
    groups = mesh.shape["date"]

    def on_device(slc, partner_offsets):
        dates = slc.shape[1] * groups
        chunks = slc.shape[3] // 16
        return pl.pallas_call(
            functools.partial(kernel, groups),
            out_shape=jax.ShapeDtypeStruct((2, 4, 1, dates), jnp.float32),
            in_specs=[pl.BlockSpec(memory_space=pltpu.HBM)] * 2,
            out_specs=pl.BlockSpec(memory_space=pltpu.VMEM),
            scratch_shapes=[
                pltpu.VMEM(slc.shape, jnp.bfloat16),
                pltpu.VMEM(partner_offsets.shape[::-1], jnp.int32),
                pltpu.VMEM((chunks // 8, 64, 128), jnp.float32),
                pltpu.VMEM((chunks, 8, 128), jnp.bfloat16),
                pltpu.VMEM((groups, 8, 128), jnp.bfloat16),
                pltpu.VMEM((groups * 8 + 4 * dates, 128), jnp.float32),
                pltpu.SemaphoreType.DMA,
                pltpu.SemaphoreType.DMA,
                pltpu.SemaphoreType.DMA,
                pltpu.SemaphoreType.DMA,
            ],
            compiler_params=pltpu.CompilerParams(
                collective_id=0, has_side_effects=True, vmem_limit_bytes=VMEM_BYTES
            ),
        )(slc, partner_offsets.T)

    return jax.shard_map(
        on_device,
        mesh=mesh,
        in_specs=(P(None, "date", None, "col"), P()),
        out_specs=P(None, None, ("date", "col"), None),
        check_vma=False,
    )
```

```python
import functools

import jax
import jax.numpy as jnp
from jax import lax
from jax.experimental import pallas as pl
from jax.experimental.pallas import tpu as pltpu
from jax.sharding import PartitionSpec as P

EPSILON = 1e-06
STRIDES = 4
VMEM_BYTES = 56_545_280
DEPTH = 8
NEAR = 3
MESH = pl.DeviceIdType.MESH


def halves(value):
    high = value.astype(jnp.bfloat16)
    low = (value - high.astype(jnp.float32)).astype(jnp.bfloat16)
    return high, low


def product(left, right):
    return jnp.dot(left, right, preferred_element_type=jnp.float32)


def gram(left, right):
    return lax.dot_general(left, right, (((1,), (1,)), ((), ())), preferred_element_type=jnp.float32)


def squared(real, imag):
    real_high, real_low = halves(real)
    imag_high, imag_low = halves(imag)
    sum_high = (real + imag).astype(jnp.bfloat16)
    less_high, less_low = halves(real - imag)
    mixed = product(real_high, imag_high) + product(real_high, imag_low) + product(real_low, imag_high)
    part = product(sum_high, less_low) + mixed
    return product(sum_high, less_high) + (part + part.T), mixed - mixed.T


def applied(real, imag, rows):
    count = rows.shape[0]
    half = count // 2
    high, low = halves(rows)
    stacked = jnp.concatenate([high, low], axis=0)
    by_real = product(stacked, real[0])
    by_imag = product(stacked, imag[0])
    by_real = by_real[:count] + by_real[count:] + product(high, real[1])
    by_imag = by_imag[:count] + by_imag[count:] + product(high, imag[1])
    return jnp.concatenate([by_real[:half] + by_imag[half:], by_real[half:] - by_imag[:half]], axis=0)


def coherences(images, pairs, diagonal):
    turned = jnp.concatenate([images[:, 64:], -images[:, :64]], axis=1)
    cov_real = gram(images, images) * (1.0 / 64.0)
    cov_imag = gram(turned, images) * (1.0 / 64.0)
    only = jnp.where(diagonal, cov_real, 0.0)
    scale_row = lax.rsqrt(jnp.sum(only, axis=0, keepdims=True) + EPSILON)
    scale_col = lax.rsqrt(jnp.sum(only, axis=1, keepdims=True) + EPSILON)
    weight = pairs * scale_row * scale_col
    return jnp.where(diagonal, 1.0, cov_real * weight), cov_imag * weight


def times_ones(real, imag):
    return jnp.sum(real, axis=0, keepdims=True), -jnp.sum(imag, axis=0, keepdims=True)


def mean_product(a, b):
    return jnp.mean(a[0] * b[0] + a[1] * b[1], axis=1, keepdims=True)


def folded(tail, means):
    for mean in means:
        tail = mean + EPSILON * tail
    return tail


def linked_phases(images, pairs):
    dates = pairs.shape[0]
    row = lax.broadcasted_iota(jnp.int32, (dates, dates), 0)
    col = lax.broadcasted_iota(jnp.int32, (dates, dates), 1)
    first = [coherences(image, pairs, row == col) for image in images]
    second = [squared(*matrix) for matrix in first]
    two = [times_ones(*matrix) for matrix in second]
    fourth = [squared(*matrix) for matrix in second]
    four = [times_ones(*matrix) for matrix in fourth]
    fourth = [(halves(real), halves(imag)) for real, imag in fourth]
    ones = jnp.ones((1, dates), jnp.float32), jnp.zeros((1, dates), jnp.float32)
    pad = jnp.zeros((2, dates), jnp.float32)
    rows, tails = [], []
    for a, b in zip(two, four):
        means = [mean_product(ones, a), mean_product(a, a), mean_product(a, b), mean_product(b, b)]
        rows.append(jnp.concatenate([b[0], a[0], pad, b[1], a[1], pad], axis=0))
        tails.append(folded(1.0, means))
    for _ in range(STRIDES):
        after = [applied(*matrix, value) for matrix, value in zip(fourth, rows)]
        for pixel in range(len(rows)):
            old, new, scale = rows[pixel], after[pixel], lax.rsqrt(tails[pixel])
            rows[pixel] = new * scale
            k = old[0:1] * scale, old[4:5] * scale
            a, b = (rows[pixel][1:2], rows[pixel][5:6]), (rows[pixel][0:1], rows[pixel][4:5])
            means = [mean_product(k, a), mean_product(a, a), mean_product(a, b), mean_product(b, b)]
            tails[pixel] = folded(1.0, means)
    rows = [value * lax.rsqrt(tail) for value, tail in zip(rows, tails)]
    return [(value[0:1], value[4:5]) for value in rows]


def pair_mask(offsets):
    slots, dates = offsets.shape
    row = lax.broadcasted_iota(jnp.int32, (dates, dates), 0)
    col = lax.broadcasted_iota(jnp.int32, (dates, dates), 1)
    apart = jnp.where(row > col, row - col, -1)
    lower = jnp.zeros((dates, dates), jnp.float32)
    for slot in range(slots):
        lower = jnp.where(offsets[slot : slot + 1, :] == apart, 1.0, lower)
    return lower + lower.T


def kernel(
    groups,
    slc_ref,
    offsets_ref,
    out_ref,
    strip,
    table,
    wide,
    outgoing,
    arrived,
    ordered,
    strip_sem,
    table_sem,
    send_sem,
    recv_sem,
    other,
):
    date = lax.axis_index("date")
    core = lax.axis_index("col")
    chunks = outgoing.shape[0]
    owners = chunks // 2
    side = date // owners
    own = side == core

    barrier = pltpu.get_barrier_semaphore()

    late = (lax.rem(date, DEPTH) >= NEAR).astype(jnp.int32)
    early_devices = 2 * NEAR * (groups // DEPTH)
    alike = jnp.where(core == 0, early_devices, 2 * groups - early_devices)

    def signal(semaphore, target):
        pl.semaphore_signal(semaphore, inc=1, device_id=target, device_id_type=MESH)

    load_strip = pltpu.make_async_copy(slc_ref, strip, strip_sem)
    load_strip.start()
    load_table = pltpu.make_async_copy(offsets_ref, table, table_sem)
    load_table.start()

    def greet(step, carry):
        signal(barrier, (lax.rem(date + step, groups), late))
        return carry

    lax.fori_loop(1, groups, greet, 0)

    @pl.when(late != core)
    def _():
        greet(0, 0)

    @pl.when(late == core)
    def _():
        signal(barrier, (date, 1 - core))

    load_strip.wait()
    lane = lax.broadcasted_iota(jnp.int32, (8, 128), 1)

    def regroup(tile, carry):
        columns = pl.ds(pl.multiple_of(tile * 128, 128), 128)
        for part in range(2):
            for t in range(2):
                wide[tile, pl.ds(part * 32 + t * 16, 16), :] = strip[part, t, :, columns].astype(jnp.float32)
        group = [wide[tile, pl.ds((g // 4) * 32 + g % 4, 8, stride=4), :] for g in range(8)]
        for bit in range(3):
            shift = 16 << bit
            upper = (lane & shift) != 0
            for g in range(8):
                other = g | (1 << bit)
                if other != g:
                    low, high = group[g], group[other]
                    group[g] = jnp.where(upper, pltpu.roll(high, shift, 1), low)
                    group[other] = jnp.where(upper, high, pltpu.roll(low, 128 - shift, 1))
        for g in range(8):
            outgoing[tile * 8 + g] = group[g].astype(jnp.bfloat16)
        return carry

    lax.fori_loop(0, chunks // 8, regroup, 0, unroll=8)

    def count():
        pl.semaphore_wait(barrier, jnp.where(late == core, alike - 1, alike + 1))
        signal(other, (date, 1 - core))

    def send(step, which):
        depth = (NEAR, DEPTH - NEAR)[which]
        first = (0, NEAR)[which]
        z, y, x = first + lax.rem(step // 2, depth), lax.rem(step // (2 * depth), 4), step // (8 * depth)
        chunk = ((x * 4 + y) * DEPTH + z) * 2 + lax.rem(step, 2)
        owner = owners * core + chunk // 2
        owner_core = lax.rem(chunk, 2)
        stays = (owner == date) & (owner_core == core)

        @pl.when(jnp.logical_not(stays))
        def _():
            pltpu.make_async_remote_copy(
                src_ref=outgoing.at[chunk],
                dst_ref=arrived.at[date],
                send_sem=send_sem,
                recv_sem=recv_sem,
                device_id=(owner, owner_core),
                device_id_type=MESH,
            ).start()

        @pl.when(stays)
        def _():
            pltpu.make_async_copy(outgoing.at[chunk], arrived.at[date], recv_sem).start()

    def send_all(which):
        def body(step, carry):
            send(step, which)
            return carry

        lax.fori_loop(0, 16 * (NEAR, DEPTH - NEAR)[which], body, 0)

    @pl.when(core == 0)
    def _():
        count()

    @pl.when(core == 1)
    def _():
        pl.semaphore_wait(other, 1)

    send_all(0)

    @pl.when(core == 0)
    def _():
        pl.semaphore_wait(other, 1)

    @pl.when(core == 1)
    def _():
        count()

    send_all(1)

    load_table.wait()
    pairs = pair_mask(table[...])

    pltpu.make_async_copy(arrived, arrived, recv_sem).wait()
    wide_rows = arrived[...].astype(jnp.float32).reshape(groups * 8, 128)
    ordered[0 : groups * 8, :] = wide_rows
    for pixel in range(4):
        for t in range(2):
            picked = ordered[pl.ds(t * 4 + pixel, groups, stride=8), :]
            ordered[pl.ds(groups * 8 + pixel * 2 * groups + t, groups, stride=2), :] = picked
    images = []
    for pixel in range(4):
        first = groups * 8 + pixel * 2 * groups
        images.append(ordered[first : first + 2 * groups, :].astype(jnp.bfloat16))
    for pixel, (real, imag) in enumerate(linked_phases(images, pairs)):
        out_ref[0, pixel] = real
        out_ref[1, pixel] = imag

    @pl.when(own)
    def _():
        rest = outgoing.at[pl.ds(0, chunks - 1)]
        pltpu.make_async_copy(rest, rest, send_sem).wait()

    @pl.when(jnp.logical_not(own))
    def _():
        pltpu.make_async_copy(outgoing, outgoing, send_sem).wait()


def solution(mesh):
    groups = mesh.shape["date"]

    def on_device(slc, partner_offsets):
        dates = slc.shape[1] * groups
        chunks = slc.shape[3] // 16
        return pl.pallas_call(
            functools.partial(kernel, groups),
            out_shape=jax.ShapeDtypeStruct((2, 4, 1, dates), jnp.float32),
            in_specs=[pl.BlockSpec(memory_space=pltpu.HBM)] * 2,
            out_specs=pl.BlockSpec(memory_space=pltpu.VMEM),
            scratch_shapes=[
                pltpu.VMEM(slc.shape, jnp.bfloat16),
                pltpu.VMEM(partner_offsets.shape[::-1], jnp.int32),
                pltpu.VMEM((chunks // 8, 64, 128), jnp.float32),
                pltpu.VMEM((chunks, 8, 128), jnp.bfloat16),
                pltpu.VMEM((groups, 8, 128), jnp.bfloat16),
                pltpu.VMEM((groups * 8 + 4 * dates, 128), jnp.float32),
                pltpu.SemaphoreType.DMA,
                pltpu.SemaphoreType.DMA,
                pltpu.SemaphoreType.DMA,
                pltpu.SemaphoreType.DMA,
                pltpu.SemaphoreType.REGULAR,
            ],
            compiler_params=pltpu.CompilerParams(
                collective_id=0, has_side_effects=True, vmem_limit_bytes=VMEM_BYTES
            ),
        )(slc, partner_offsets.T)

    return jax.shard_map(
        on_device,
        mesh=mesh,
        in_specs=(P(None, "date", None, "col"), P()),
        out_specs=P(None, None, ("date", "col"), None),
        check_vma=False,
    )
```

```python
import functools

import jax
import jax.numpy as jnp
from jax import lax
from jax.experimental import pallas as pl
from jax.experimental.pallas import tpu as pltpu
from jax.sharding import PartitionSpec as P

EPSILON = 1e-06
STRIDES = 4
VMEM_BYTES = 56_545_280
DEPTH = 8
NEAR = 3
MESH = pl.DeviceIdType.MESH


def halves(value):
    high = value.astype(jnp.bfloat16)
    low = (value - high.astype(jnp.float32)).astype(jnp.bfloat16)
    return high, low


def product(left, right):
    return jnp.dot(left, right, preferred_element_type=jnp.float32)


def gram(left, right):
    return lax.dot_general(left, right, (((1,), (1,)), ((), ())), preferred_element_type=jnp.float32)


def squared(real, imag):
    real_high, real_low = halves(real)
    imag_high, imag_low = halves(imag)
    sum_high = (real + imag).astype(jnp.bfloat16)
    less_high, less_low = halves(real - imag)
    mixed = product(real_high, imag_high) + product(real_high, imag_low) + product(real_low, imag_high)
    part = product(sum_high, less_low) + mixed
    return product(sum_high, less_high) + (part + part.T), mixed - mixed.T


def applied(real, imag, rows):
    count = rows.shape[0]
    half = count // 2
    high, low = halves(rows)
    stacked = jnp.concatenate([high, low], axis=0)
    by_real = product(stacked, real[0])
    by_imag = product(stacked, imag[0])
    by_real = by_real[:count] + by_real[count:] + product(high, real[1])
    by_imag = by_imag[:count] + by_imag[count:] + product(high, imag[1])
    return jnp.concatenate([by_real[:half] + by_imag[half:], by_real[half:] - by_imag[:half]], axis=0)


def coherences(images, pairs, diagonal):
    turned = jnp.concatenate([images[:, 64:], -images[:, :64]], axis=1)
    cov_real = gram(images, images) * (1.0 / 64.0)
    cov_imag = gram(turned, images) * (1.0 / 64.0)
    only = jnp.where(diagonal, cov_real, 0.0)
    scale_row = lax.rsqrt(jnp.sum(only, axis=0, keepdims=True) + EPSILON)
    scale_col = lax.rsqrt(jnp.sum(only, axis=1, keepdims=True) + EPSILON)
    weight = pairs * scale_row * scale_col
    return jnp.where(diagonal, 1.0, cov_real * weight), cov_imag * weight


def times_ones(real, imag):
    return jnp.sum(real, axis=0, keepdims=True), -jnp.sum(imag, axis=0, keepdims=True)


def mean_product(a, b):
    return jnp.mean(a[0] * b[0] + a[1] * b[1], axis=1, keepdims=True)


def folded(tail, means):
    for mean in means:
        tail = mean + EPSILON * tail
    return tail


def linked_phases(images, pairs):
    dates = pairs.shape[0]
    row = lax.broadcasted_iota(jnp.int32, (dates, dates), 0)
    col = lax.broadcasted_iota(jnp.int32, (dates, dates), 1)
    first = [coherences(image, pairs, row == col) for image in images]
    second = [squared(*matrix) for matrix in first]
    two = [times_ones(*matrix) for matrix in second]
    fourth = [squared(*matrix) for matrix in second]
    four = [times_ones(*matrix) for matrix in fourth]
    fourth = [(halves(real), halves(imag)) for real, imag in fourth]
    ones = jnp.ones((1, dates), jnp.float32), jnp.zeros((1, dates), jnp.float32)
    pad = jnp.zeros((2, dates), jnp.float32)
    rows, tails = [], []
    for a, b in zip(two, four):
        means = [mean_product(ones, a), mean_product(a, a), mean_product(a, b), mean_product(b, b)]
        rows.append(jnp.concatenate([b[0], a[0], pad, b[1], a[1], pad], axis=0))
        tails.append(folded(1.0, means))
    for _ in range(STRIDES):
        after = [applied(*matrix, value) for matrix, value in zip(fourth, rows)]
        for pixel in range(len(rows)):
            old, new, scale = rows[pixel], after[pixel], lax.rsqrt(tails[pixel])
            rows[pixel] = new * scale
            k = old[0:1] * scale, old[4:5] * scale
            a, b = (rows[pixel][1:2], rows[pixel][5:6]), (rows[pixel][0:1], rows[pixel][4:5])
            means = [mean_product(k, a), mean_product(a, a), mean_product(a, b), mean_product(b, b)]
            tails[pixel] = folded(1.0, means)
    rows = [value * lax.rsqrt(tail) for value, tail in zip(rows, tails)]
    return [(value[0:1], value[4:5]) for value in rows]


def pair_mask(offsets):
    slots, dates = offsets.shape
    row = lax.broadcasted_iota(jnp.int32, (dates, dates), 0)
    col = lax.broadcasted_iota(jnp.int32, (dates, dates), 1)
    apart = jnp.where(row > col, row - col, -1)
    lower = jnp.zeros((dates, dates), jnp.float32)
    for slot in range(slots):
        lower = jnp.where(offsets[slot : slot + 1, :] == apart, 1.0, lower)
    return lower + lower.T


def kernel(
    groups,
    slc_ref,
    offsets_ref,
    out_ref,
    strip,
    table,
    wide,
    outgoing,
    arrived,
    ordered,
    strip_sem,
    table_sem,
    send_sem,
    recv_sem,
    other,
):
    date = lax.axis_index("date")
    core = lax.axis_index("col")
    chunks = outgoing.shape[0]
    owners = chunks // 2
    side = date // owners
    own = side == core

    barrier = pltpu.get_barrier_semaphore()

    late = (lax.rem(date, DEPTH) >= NEAR).astype(jnp.int32)
    early_devices = 2 * NEAR * (groups // DEPTH)
    alike = jnp.where(core == 0, early_devices, 2 * groups - early_devices)

    def signal(semaphore, target):
        pl.semaphore_signal(semaphore, inc=1, device_id=target, device_id_type=MESH)

    load_strip = pltpu.make_async_copy(slc_ref, strip, strip_sem)
    load_strip.start()
    load_table = pltpu.make_async_copy(offsets_ref, table, table_sem)
    load_table.start()

    def greet(step, carry):
        signal(barrier, (lax.rem(date + step, groups), late))
        return carry

    rest = (groups - 1) % 16
    for step in range(1, 1 + rest):
        greet(step, 0)
    lax.fori_loop(1 + rest, groups, greet, 0, unroll=16)

    @pl.when(late != core)
    def _():
        greet(0, 0)

    @pl.when(late == core)
    def _():
        signal(barrier, (date, 1 - core))

    load_strip.wait()
    lane = lax.broadcasted_iota(jnp.int32, (8, 128), 1)

    def regroup(tile, carry):
        columns = pl.ds(pl.multiple_of(tile * 128, 128), 128)
        for part in range(2):
            for t in range(2):
                wide[tile, pl.ds(part * 32 + t * 16, 16), :] = strip[part, t, :, columns].astype(jnp.float32)
        group = [wide[tile, pl.ds((g // 4) * 32 + g % 4, 8, stride=4), :] for g in range(8)]
        for bit in range(3):
            shift = 16 << bit
            upper = (lane & shift) != 0
            for g in range(8):
                other = g | (1 << bit)
                if other != g:
                    low, high = group[g], group[other]
                    group[g] = jnp.where(upper, pltpu.roll(high, shift, 1), low)
                    group[other] = jnp.where(upper, high, pltpu.roll(low, 128 - shift, 1))
        for g in range(8):
            outgoing[tile * 8 + g] = group[g].astype(jnp.bfloat16)
        return carry

    lax.fori_loop(0, chunks // 8, regroup, 0, unroll=8)

    def count():
        pl.semaphore_wait(barrier, jnp.where(late == core, alike - 1, alike + 1))
        signal(other, (date, 1 - core))

    def send(step, which):
        depth = (NEAR, DEPTH - NEAR)[which]
        first = (0, NEAR)[which]
        z, y, x = first + lax.rem(step // 2, depth), lax.rem(step // (2 * depth), 4), step // (8 * depth)
        chunk = ((x * 4 + y) * DEPTH + z) * 2 + lax.rem(step, 2)
        owner = owners * core + chunk // 2
        owner_core = lax.rem(chunk, 2)
        stays = (owner == date) & (owner_core == core)

        @pl.when(jnp.logical_not(stays))
        def _():
            pltpu.make_async_remote_copy(
                src_ref=outgoing.at[chunk],
                dst_ref=arrived.at[date],
                send_sem=send_sem,
                recv_sem=recv_sem,
                device_id=(owner, owner_core),
                device_id_type=MESH,
            ).start()

        @pl.when(stays)
        def _():
            pltpu.make_async_copy(outgoing.at[chunk], arrived.at[date], recv_sem).start()

    def send_all(which):
        def body(step, carry):
            send(step, which)
            return carry

        lax.fori_loop(0, 16 * (NEAR, DEPTH - NEAR)[which], body, 0)

    @pl.when(core == 0)
    def _():
        count()

    @pl.when(core == 1)
    def _():
        pl.semaphore_wait(other, 1)

    send_all(0)

    @pl.when(core == 0)
    def _():
        pl.semaphore_wait(other, 1)

    @pl.when(core == 1)
    def _():
        count()

    send_all(1)

    load_table.wait()
    pairs = pair_mask(table[...])

    pltpu.make_async_copy(arrived, arrived, recv_sem).wait()
    wide_rows = arrived[...].astype(jnp.float32).reshape(groups * 8, 128)
    ordered[0 : groups * 8, :] = wide_rows
    for pixel in range(4):
        for t in range(2):
            picked = ordered[pl.ds(t * 4 + pixel, groups, stride=8), :]
            ordered[pl.ds(groups * 8 + pixel * 2 * groups + t, groups, stride=2), :] = picked
    images = []
    for pixel in range(4):
        first = groups * 8 + pixel * 2 * groups
        images.append(ordered[first : first + 2 * groups, :].astype(jnp.bfloat16))
    for pixel, (real, imag) in enumerate(linked_phases(images, pairs)):
        out_ref[0, pixel] = real
        out_ref[1, pixel] = imag

    @pl.when(own)
    def _():
        rest = outgoing.at[pl.ds(0, chunks - 1)]
        pltpu.make_async_copy(rest, rest, send_sem).wait()

    @pl.when(jnp.logical_not(own))
    def _():
        pltpu.make_async_copy(outgoing, outgoing, send_sem).wait()


def solution(mesh):
    groups = mesh.shape["date"]

    def on_device(slc, partner_offsets):
        dates = slc.shape[1] * groups
        chunks = slc.shape[3] // 16
        return pl.pallas_call(
            functools.partial(kernel, groups),
            out_shape=jax.ShapeDtypeStruct((2, 4, 1, dates), jnp.float32),
            in_specs=[pl.BlockSpec(memory_space=pltpu.HBM)] * 2,
            out_specs=pl.BlockSpec(memory_space=pltpu.VMEM),
            scratch_shapes=[
                pltpu.VMEM(slc.shape, jnp.bfloat16),
                pltpu.VMEM(partner_offsets.shape[::-1], jnp.int32),
                pltpu.VMEM((chunks // 8, 64, 128), jnp.float32),
                pltpu.VMEM((chunks, 8, 128), jnp.bfloat16),
                pltpu.VMEM((groups, 8, 128), jnp.bfloat16),
                pltpu.VMEM((groups * 8 + 4 * dates, 128), jnp.float32),
                pltpu.SemaphoreType.DMA,
                pltpu.SemaphoreType.DMA,
                pltpu.SemaphoreType.DMA,
                pltpu.SemaphoreType.DMA,
                pltpu.SemaphoreType.REGULAR,
            ],
            compiler_params=pltpu.CompilerParams(
                collective_id=0, has_side_effects=True, vmem_limit_bytes=VMEM_BYTES
            ),
        )(slc, partner_offsets.T)

    return jax.shard_map(
        on_device,
        mesh=mesh,
        in_specs=(P(None, "date", None, "col"), P()),
        out_specs=P(None, None, ("date", "col"), None),
        check_vma=False,
    )
```

```python
import functools

import jax
import jax.numpy as jnp
from jax import lax
from jax.experimental import pallas as pl
from jax.experimental.pallas import tpu as pltpu
from jax.sharding import PartitionSpec as P

EPSILON = 1e-06
STRIDES = 4
VMEM_BYTES = 56_545_280
DEPTH = 8
NEAR = 3
MESH = pl.DeviceIdType.MESH


def halves(value):
    high = value.astype(jnp.bfloat16)
    low = (value - high.astype(jnp.float32)).astype(jnp.bfloat16)
    return high, low


def product(left, right):
    return jnp.dot(left, right, preferred_element_type=jnp.float32)


def gram(left, right):
    return lax.dot_general(left, right, (((1,), (1,)), ((), ())), preferred_element_type=jnp.float32)


def squared(real, imag):
    real_high, real_low = halves(real)
    imag_high, imag_low = halves(imag)
    sum_high = (real + imag).astype(jnp.bfloat16)
    less_high, less_low = halves(real - imag)
    mixed = product(real_high, imag_high) + product(real_high, imag_low) + product(real_low, imag_high)
    part = product(sum_high, less_low) + mixed
    return product(sum_high, less_high) + (part + part.T), mixed - mixed.T


def applied(real, imag, rows):
    count = rows.shape[0]
    half = count // 2
    high, low = halves(rows)
    stacked = jnp.concatenate([high, low], axis=0)
    by_real = product(stacked, real[0])
    by_imag = product(stacked, imag[0])
    by_real = by_real[:count] + by_real[count:] + product(high, real[1])
    by_imag = by_imag[:count] + by_imag[count:] + product(high, imag[1])
    return jnp.concatenate([by_real[:half] + by_imag[half:], by_real[half:] - by_imag[:half]], axis=0)


def coherences(images, pairs, diagonal):
    turned = jnp.concatenate([images[:, 64:], -images[:, :64]], axis=1)
    cov_real = gram(images, images) * (1.0 / 64.0)
    cov_imag = gram(turned, images) * (1.0 / 64.0)
    only = jnp.where(diagonal, cov_real, 0.0)
    scale_row = lax.rsqrt(jnp.sum(only, axis=0, keepdims=True) + EPSILON)
    scale_col = lax.rsqrt(jnp.sum(only, axis=1, keepdims=True) + EPSILON)
    weight = pairs * scale_row * scale_col
    return jnp.where(diagonal, 1.0, cov_real * weight), cov_imag * weight


def times_ones(real, imag):
    return jnp.sum(real, axis=0, keepdims=True), -jnp.sum(imag, axis=0, keepdims=True)


def mean_product(a, b):
    return jnp.mean(a[0] * b[0] + a[1] * b[1], axis=1, keepdims=True)


def folded(tail, means):
    for mean in means:
        tail = mean + EPSILON * tail
    return tail


def linked_phases(images, pairs):
    dates = pairs.shape[0]
    row = lax.broadcasted_iota(jnp.int32, (dates, dates), 0)
    col = lax.broadcasted_iota(jnp.int32, (dates, dates), 1)
    first = [coherences(image, pairs, row == col) for image in images]
    second = [squared(*matrix) for matrix in first]
    two = [times_ones(*matrix) for matrix in second]
    fourth = [squared(*matrix) for matrix in second]
    four = [times_ones(*matrix) for matrix in fourth]
    fourth = [(halves(real), halves(imag)) for real, imag in fourth]
    ones = jnp.ones((1, dates), jnp.float32), jnp.zeros((1, dates), jnp.float32)
    pad = jnp.zeros((2, dates), jnp.float32)
    rows, tails = [], []
    for a, b in zip(two, four):
        means = [mean_product(ones, a), mean_product(a, a), mean_product(a, b), mean_product(b, b)]
        rows.append(jnp.concatenate([b[0], a[0], pad, b[1], a[1], pad], axis=0))
        tails.append(folded(1.0, means))
    for _ in range(STRIDES):
        after = [applied(*matrix, value) for matrix, value in zip(fourth, rows)]
        for pixel in range(len(rows)):
            old, new, scale = rows[pixel], after[pixel], lax.rsqrt(tails[pixel])
            rows[pixel] = new * scale
            k = old[0:1] * scale, old[4:5] * scale
            a, b = (rows[pixel][1:2], rows[pixel][5:6]), (rows[pixel][0:1], rows[pixel][4:5])
            means = [mean_product(k, a), mean_product(a, a), mean_product(a, b), mean_product(b, b)]
            tails[pixel] = folded(1.0, means)
    rows = [value * lax.rsqrt(tail) for value, tail in zip(rows, tails)]
    return [(value[0:1], value[4:5]) for value in rows]


def pair_mask(offsets):
    slots, dates = offsets.shape
    row = lax.broadcasted_iota(jnp.int32, (dates, dates), 0)
    col = lax.broadcasted_iota(jnp.int32, (dates, dates), 1)
    apart = jnp.where(row > col, row - col, -1)
    lower = jnp.zeros((dates, dates), jnp.float32)
    for slot in range(slots):
        lower = jnp.where(offsets[slot : slot + 1, :] == apart, 1.0, lower)
    return lower + lower.T


def kernel(
    groups,
    slc_ref,
    offsets_ref,
    out_ref,
    strip,
    table,
    wide,
    outgoing,
    arrived,
    ordered,
    strip_sem,
    table_sem,
    send_sem,
    recv_sem,
    other,
):
    date = lax.axis_index("date")
    core = lax.axis_index("col")
    chunks = outgoing.shape[0]
    owners = chunks // 2
    side = date // owners
    own = side == core

    barrier = pltpu.get_barrier_semaphore()

    late = (lax.rem(date, DEPTH) >= NEAR).astype(jnp.int32)
    early_devices = 2 * NEAR * (groups // DEPTH)
    alike = jnp.where(core == 0, early_devices, 2 * groups - early_devices)

    def signal(semaphore, target):
        pl.semaphore_signal(semaphore, inc=1, device_id=target, device_id_type=MESH)

    load_strip = pltpu.make_async_copy(slc_ref, strip, strip_sem)
    load_strip.start()
    load_table = pltpu.make_async_copy(offsets_ref, table, table_sem)
    load_table.start()

    def greet(step, carry):
        signal(barrier, (lax.rem(date + step, groups), late))
        return carry

    rest = (groups - 1) % 16
    for step in range(1, 1 + rest):
        greet(step, 0)
    lax.fori_loop(1 + rest, groups, greet, 0, unroll=16)

    @pl.when(late != core)
    def _():
        greet(0, 0)

    @pl.when(late == core)
    def _():
        signal(barrier, (date, 1 - core))

    load_strip.wait()
    lane = lax.broadcasted_iota(jnp.int32, (8, 128), 1)

    def regroup(tile, carry):
        columns = pl.ds(pl.multiple_of(tile * 128, 128), 128)
        for part in range(2):
            for t in range(2):
                wide[tile, pl.ds(part * 32 + t * 16, 16), :] = strip[part, t, :, columns].astype(jnp.float32)
        group = [wide[tile, pl.ds((g // 4) * 32 + g % 4, 8, stride=4), :] for g in range(8)]
        for bit in range(3):
            shift = 16 << bit
            upper = (lane & shift) != 0
            for g in range(8):
                other = g | (1 << bit)
                if other != g:
                    low, high = group[g], group[other]
                    group[g] = jnp.where(upper, pltpu.roll(high, shift, 1), low)
                    group[other] = jnp.where(upper, high, pltpu.roll(low, 128 - shift, 1))
        for g in range(8):
            outgoing[tile * 8 + g] = group[g].astype(jnp.bfloat16)
        return carry

    lax.fori_loop(0, chunks // 8, regroup, 0, unroll=8)

    def count():
        pl.semaphore_wait(barrier, jnp.where(late == core, alike - 1, alike + 1))
        signal(other, (date, 1 - core))

    def send(step, which):
        depth = (NEAR, DEPTH - NEAR)[which]
        first = (0, NEAR)[which]
        z, y, x = first + lax.rem(step // 2, depth), lax.rem(step // (2 * depth), 4), step // (8 * depth)
        chunk = ((x * 4 + y) * DEPTH + z) * 2 + lax.rem(step, 2)
        owner = owners * core + chunk // 2
        owner_core = lax.rem(chunk, 2)
        stays = (owner == date) & (owner_core == core)

        @pl.when(jnp.logical_not(stays))
        def _():
            pltpu.make_async_remote_copy(
                src_ref=outgoing.at[chunk],
                dst_ref=arrived.at[date],
                send_sem=send_sem,
                recv_sem=recv_sem,
                device_id=(owner, owner_core),
                device_id_type=MESH,
            ).start()

        @pl.when(stays)
        def _():
            pltpu.make_async_copy(outgoing.at[chunk], arrived.at[date], recv_sem).start()

    def send_all(which):
        def body(step, carry):
            send(step, which)
            return carry

        lax.fori_loop(0, 16 * (NEAR, DEPTH - NEAR)[which], body, 0)

    @pl.when(core == 0)
    def _():
        count()

    @pl.when(core == 1)
    def _():
        pl.semaphore_wait(other, 1)

    send_all(0)

    @pl.when(core == 0)
    def _():
        pl.semaphore_wait(other, 1)

    @pl.when(core == 1)
    def _():
        count()

    send_all(1)

    load_table.wait()
    pairs = pair_mask(table[...])

    pltpu.make_async_copy(arrived, arrived, recv_sem).wait()
    wide_rows = arrived[...].astype(jnp.float32).reshape(groups * 8, 128)
    ordered[0 : groups * 8, :] = wide_rows
    for pixel in range(4):
        for t in range(2):
            picked = ordered[pl.ds(t * 4 + pixel, groups, stride=8), :]
            ordered[pl.ds(groups * 8 + pixel * 2 * groups + t, groups, stride=2), :] = picked
    images = []
    for pixel in range(4):
        first = groups * 8 + pixel * 2 * groups
        images.append(ordered[first : first + 2 * groups, :].astype(jnp.bfloat16))
    for pixel, (real, imag) in enumerate(linked_phases(images, pairs)):
        out_ref[0, pixel] = real
        out_ref[1, pixel] = imag

    @pl.when(own)
    def _():
        rest = outgoing.at[pl.ds(0, chunks - 1)]
        pltpu.make_async_copy(rest, rest, send_sem).wait()

    @pl.when(jnp.logical_not(own))
    def _():
        pltpu.make_async_copy(outgoing, outgoing, send_sem).wait()


def solution(mesh):
    groups = mesh.shape["date"]

    def on_device(slc, partner_offsets):
        dates = slc.shape[1] * groups
        chunks = slc.shape[3] // 16
        return pl.pallas_call(
            functools.partial(kernel, groups),
            out_shape=jax.ShapeDtypeStruct((2, 4, 1, dates), jnp.float32),
            in_specs=[pl.BlockSpec(memory_space=pltpu.HBM)] * 2,
            out_specs=pl.BlockSpec(memory_space=pltpu.VMEM),
            scratch_shapes=[
                pltpu.VMEM(slc.shape, jnp.bfloat16),
                pltpu.VMEM(partner_offsets.shape[::-1], jnp.int32),
                pltpu.VMEM((chunks // 8 + 1, 64, 128), jnp.float32),
                pltpu.VMEM((chunks, 8, 128), jnp.bfloat16),
                pltpu.VMEM((groups, 8, 128), jnp.bfloat16),
                pltpu.VMEM((groups * 8 + 4 * dates + 8, 128), jnp.float32),
                pltpu.SemaphoreType.DMA,
                pltpu.SemaphoreType.DMA,
                pltpu.SemaphoreType.DMA,
                pltpu.SemaphoreType.DMA,
                pltpu.SemaphoreType.REGULAR,
            ],
            compiler_params=pltpu.CompilerParams(
                collective_id=0, has_side_effects=True, vmem_limit_bytes=VMEM_BYTES
            ),
        )(slc, partner_offsets.T)

    return jax.shard_map(
        on_device,
        mesh=mesh,
        in_specs=(P(None, "date", None, "col"), P()),
        out_specs=P(None, None, ("date", "col"), None),
        check_vma=False,
    )
```

```python
import functools

import jax
import jax.numpy as jnp
from jax import lax
from jax.experimental import pallas as pl
from jax.experimental.pallas import tpu as pltpu
from jax.sharding import PartitionSpec as P

EPSILON = 1e-06
STRIDES = 4
VMEM_BYTES = 56_545_280
DEPTH = 8
NEAR = 3
MESH = pl.DeviceIdType.MESH


def halves(value):
    high = value.astype(jnp.bfloat16)
    low = (value - high.astype(jnp.float32)).astype(jnp.bfloat16)
    return high, low


def product(left, right):
    return jnp.dot(left, right, preferred_element_type=jnp.float32)


def gram(left, right):
    return lax.dot_general(left, right, (((1,), (1,)), ((), ())), preferred_element_type=jnp.float32)


def squared(real, imag):
    real_high, real_low = halves(real)
    imag_high, imag_low = halves(imag)
    sum_high = (real + imag).astype(jnp.bfloat16)
    less_high, less_low = halves(real - imag)
    mixed = product(real_high, imag_high) + product(real_high, imag_low) + product(real_low, imag_high)
    part = product(sum_high, less_low) + mixed
    return product(sum_high, less_high) + (part + part.T), mixed - mixed.T


def applied(real, imag, rows):
    count = rows.shape[0]
    half = count // 2
    high, low = halves(rows)
    stacked = jnp.concatenate([high, low], axis=0)
    by_real = product(stacked, real[0])
    by_imag = product(stacked, imag[0])
    by_real = by_real[:count] + by_real[count:] + product(high, real[1])
    by_imag = by_imag[:count] + by_imag[count:] + product(high, imag[1])
    return jnp.concatenate([by_real[:half] + by_imag[half:], by_real[half:] - by_imag[:half]], axis=0)


def coherences(images, pairs, diagonal):
    turned = jnp.concatenate([images[:, 64:], -images[:, :64]], axis=1)
    cov_real = gram(images, images) * (1.0 / 64.0)
    cov_imag = gram(turned, images) * (1.0 / 64.0)
    only = jnp.where(diagonal, cov_real, 0.0)
    scale_row = lax.rsqrt(jnp.sum(only, axis=0, keepdims=True) + EPSILON)
    scale_col = lax.rsqrt(jnp.sum(only, axis=1, keepdims=True) + EPSILON)
    weight = pairs * scale_row * scale_col
    return jnp.where(diagonal, 1.0, cov_real * weight), cov_imag * weight


def times_ones(real, imag):
    return jnp.sum(real, axis=0, keepdims=True), -jnp.sum(imag, axis=0, keepdims=True)


def mean_product(a, b):
    return jnp.mean(a[0] * b[0] + a[1] * b[1], axis=1, keepdims=True)


def folded(tail, means):
    for mean in means:
        tail = mean + EPSILON * tail
    return tail


def linked_phases(images, pairs):
    dates = pairs.shape[0]
    row = lax.broadcasted_iota(jnp.int32, (dates, dates), 0)
    col = lax.broadcasted_iota(jnp.int32, (dates, dates), 1)
    first = [coherences(image, pairs, row == col) for image in images]
    second = [squared(*matrix) for matrix in first]
    two = [times_ones(*matrix) for matrix in second]
    fourth = [squared(*matrix) for matrix in second]
    four = [times_ones(*matrix) for matrix in fourth]
    fourth = [(halves(real), halves(imag)) for real, imag in fourth]
    ones = jnp.ones((1, dates), jnp.float32), jnp.zeros((1, dates), jnp.float32)
    pad = jnp.zeros((2, dates), jnp.float32)
    rows, tails = [], []
    for a, b in zip(two, four):
        means = [mean_product(ones, a), mean_product(a, a), mean_product(a, b), mean_product(b, b)]
        rows.append(jnp.concatenate([b[0], a[0], pad, b[1], a[1], pad], axis=0))
        tails.append(folded(1.0, means))
    for _ in range(STRIDES):
        after = [applied(*matrix, value) for matrix, value in zip(fourth, rows)]
        for pixel in range(len(rows)):
            old, new, scale = rows[pixel], after[pixel], lax.rsqrt(tails[pixel])
            rows[pixel] = new * scale
            k = old[0:1] * scale, old[4:5] * scale
            a, b = (rows[pixel][1:2], rows[pixel][5:6]), (rows[pixel][0:1], rows[pixel][4:5])
            means = [mean_product(k, a), mean_product(a, a), mean_product(a, b), mean_product(b, b)]
            tails[pixel] = folded(1.0, means)
    rows = [value * lax.rsqrt(tail) for value, tail in zip(rows, tails)]
    return [(value[0:1], value[4:5]) for value in rows]


def pair_mask(offsets):
    slots, dates = offsets.shape
    row = lax.broadcasted_iota(jnp.int32, (dates, dates), 0)
    col = lax.broadcasted_iota(jnp.int32, (dates, dates), 1)
    apart = jnp.where(row > col, row - col, -1)
    lower = jnp.zeros((dates, dates), jnp.float32)
    for slot in range(slots):
        lower = jnp.where(offsets[slot : slot + 1, :] == apart, 1.0, lower)
    return lower + lower.T


def kernel(
    groups,
    slc_ref,
    offsets_ref,
    out_ref,
    strip,
    table,
    wide,
    outgoing,
    arrived,
    ordered,
    strip_sem,
    table_sem,
    send_sem,
    recv_sem,
    other,
):
    date = lax.axis_index("date")
    core = lax.axis_index("col")
    chunks = outgoing.shape[0]
    owners = chunks // 2
    side = date // owners
    own = side == core

    barrier = pltpu.get_barrier_semaphore()

    late = (lax.rem(date, DEPTH) >= NEAR).astype(jnp.int32)
    early_devices = 2 * NEAR * (groups // DEPTH)
    alike = jnp.where(core == 0, early_devices, 2 * groups - early_devices)

    def signal(semaphore, target):
        pl.semaphore_signal(semaphore, inc=1, device_id=target, device_id_type=MESH)

    load_strip = pltpu.make_async_copy(slc_ref, strip, strip_sem)
    load_strip.start()
    load_table = pltpu.make_async_copy(offsets_ref, table, table_sem)
    load_table.start()

    def greet(step, carry):
        signal(barrier, (lax.rem(date + step, groups), late))
        return carry

    rest = (groups - 1) % 16
    for step in range(1, 1 + rest):
        greet(step, 0)
    lax.fori_loop(1 + rest, groups, greet, 0, unroll=16)

    @pl.when(late != core)
    def _():
        greet(0, 0)

    @pl.when(late == core)
    def _():
        signal(barrier, (date, 1 - core))

    load_strip.wait()
    lane = lax.broadcasted_iota(jnp.int32, (8, 128), 1)

    def regroup(tile, carry):
        columns = pl.ds(pl.multiple_of(tile * 128, 128), 128)
        for part in range(2):
            for t in range(2):
                wide[tile, pl.ds(part * 32 + t * 16, 16), :] = strip[part, t, :, columns].astype(jnp.float32)
        group = [wide[tile, pl.ds((g // 4) * 32 + g % 4, 8, stride=4), :] for g in range(8)]
        for bit in range(3):
            shift = 16 << bit
            upper = (lane & shift) != 0
            for g in range(8):
                other = g | (1 << bit)
                if other != g:
                    low, high = group[g], group[other]
                    group[g] = jnp.where(upper, pltpu.roll(high, shift, 1), low)
                    group[other] = jnp.where(upper, high, pltpu.roll(low, 128 - shift, 1))
        for g in range(8):
            outgoing[tile * 8 + g] = group[g].astype(jnp.bfloat16)
        return carry

    lax.fori_loop(0, chunks // 8, regroup, 0, unroll=8)

    def count():
        pl.semaphore_wait(barrier, jnp.where(late == core, alike - 1, alike + 1))
        signal(other, (date, 1 - core))

    def send(step, which):
        depth = (NEAR, DEPTH - NEAR)[which]
        first = (0, NEAR)[which]
        z, y, x = first + lax.rem(step // 2 + which * core, depth), lax.rem(step // (2 * depth), 4), step // (8 * depth)
        chunk = ((x * 4 + y) * DEPTH + z) * 2 + lax.rem(step, 2)
        owner = owners * core + chunk // 2
        owner_core = lax.rem(chunk, 2)
        stays = (owner == date) & (owner_core == core)

        @pl.when(jnp.logical_not(stays))
        def _():
            pltpu.make_async_remote_copy(
                src_ref=outgoing.at[chunk],
                dst_ref=arrived.at[date],
                send_sem=send_sem,
                recv_sem=recv_sem,
                device_id=(owner, owner_core),
                device_id_type=MESH,
            ).start()

        @pl.when(stays)
        def _():
            pltpu.make_async_copy(outgoing.at[chunk], arrived.at[date], recv_sem).start()

    def send_all(which):
        def body(step, carry):
            send(step, which)
            return carry

        lax.fori_loop(0, 16 * (NEAR, DEPTH - NEAR)[which], body, 0)

    @pl.when(core == 0)
    def _():
        count()

    @pl.when(core == 1)
    def _():
        pl.semaphore_wait(other, 1)

    send_all(0)

    @pl.when(core == 0)
    def _():
        pl.semaphore_wait(other, 1)

    @pl.when(core == 1)
    def _():
        count()

    send_all(1)

    load_table.wait()
    pairs = pair_mask(table[...])

    pltpu.make_async_copy(arrived, arrived, recv_sem).wait()
    wide_rows = arrived[...].astype(jnp.float32).reshape(groups * 8, 128)
    ordered[0 : groups * 8, :] = wide_rows
    for pixel in range(4):
        for t in range(2):
            picked = ordered[pl.ds(t * 4 + pixel, groups, stride=8), :]
            ordered[pl.ds(groups * 8 + pixel * 2 * groups + t, groups, stride=2), :] = picked
    images = []
    for pixel in range(4):
        first = groups * 8 + pixel * 2 * groups
        images.append(ordered[first : first + 2 * groups, :].astype(jnp.bfloat16))
    for pixel, (real, imag) in enumerate(linked_phases(images, pairs)):
        out_ref[0, pixel] = real
        out_ref[1, pixel] = imag

    @pl.when(own)
    def _():
        rest = outgoing.at[pl.ds(0, chunks - 1)]
        pltpu.make_async_copy(rest, rest, send_sem).wait()

    @pl.when(jnp.logical_not(own))
    def _():
        pltpu.make_async_copy(outgoing, outgoing, send_sem).wait()


def solution(mesh):
    groups = mesh.shape["date"]

    def on_device(slc, partner_offsets):
        dates = slc.shape[1] * groups
        chunks = slc.shape[3] // 16
        return pl.pallas_call(
            functools.partial(kernel, groups),
            out_shape=jax.ShapeDtypeStruct((2, 4, 1, dates), jnp.float32),
            in_specs=[pl.BlockSpec(memory_space=pltpu.HBM)] * 2,
            out_specs=pl.BlockSpec(memory_space=pltpu.VMEM),
            scratch_shapes=[
                pltpu.VMEM(slc.shape, jnp.bfloat16),
                pltpu.VMEM(partner_offsets.shape[::-1], jnp.int32),
                pltpu.VMEM((chunks // 8 + 1, 64, 128), jnp.float32),
                pltpu.VMEM((chunks, 8, 128), jnp.bfloat16),
                pltpu.VMEM((groups, 8, 128), jnp.bfloat16),
                pltpu.VMEM((groups * 8 + 4 * dates + 8, 128), jnp.float32),
                pltpu.SemaphoreType.DMA,
                pltpu.SemaphoreType.DMA,
                pltpu.SemaphoreType.DMA,
                pltpu.SemaphoreType.DMA,
                pltpu.SemaphoreType.REGULAR,
            ],
            compiler_params=pltpu.CompilerParams(
                collective_id=0, has_side_effects=True, vmem_limit_bytes=VMEM_BYTES
            ),
        )(slc, partner_offsets.T)

    return jax.shard_map(
        on_device,
        mesh=mesh,
        in_specs=(P(None, "date", None, "col"), P()),
        out_specs=P(None, None, ("date", "col"), None),
        check_vma=False,
    )
```
